32 devices in a mesh: win: 2 (over y), row: 16 (over z, x, core).
Axes of the slice: x: 2, y: 2, z: 4, core: 2. Of those that a mesh axis runs over, the one named last changes fastest.
Arguments:
- image: float32 [3, 2048, 4096], P(None, ('win', 'row')), parts along dimension 1, may hold values from -6 to 6
- grad_x: bfloat16 [3, 2048, 4096], P(None, ('win', 'row')), parts along dimension 1, may hold values from -6 to 6
- grad_y: bfloat16 [3, 2048, 4096], P(None, ('win', 'row')), parts along dimension 1, may hold values from -6 to 6
- classes: int32 [2048, 4096], P(('win', 'row')), parts along dimension 0, may hold values from 0 to 3
- validity: int32 [2, 4], P('win'), parts along dimension 0, may hold values 0 or 1
- owners: int32 [2, 4, 2], P('win'), parts along dimension 0, may hold values from 0 to 1
Outputs:
- solution: float32 [3, 2048, 4096], P(None, ('win', 'row')), parts along dimension 1
The draws below stay inside these ranges and needn't reach their ends.
There are 2 independent parts, one for each index of `win`. The reference program is written for one: setup_inputs(seed, part) draws one part's arguments, and reference() takes and returns one part's arrays. A program takes and returns all parts, laid end to end along the dimension named above; each array names one. Nothing has to cross between parts.
All inputs are finite; a program needn't handle non-finite values.
Results may differ from the reference program's by a relative error of at most 0.0003.
Values may be sent and summed in bfloat16 or wider, within the bound.
A program may use at most 128 MiB of HBM per device.

```python
import jax
import jax.numpy as jnp

TILE_ROWS = 1024
TILE_COLS = 1024
TILES_X = 4
BAND = 48
SWEEPS = 4
HEIGHT = 1024
WIDTH = 4096
TILES_Y = 1


def set_ends(drawn, key, least, largest):
    dims = drawn.shape
    place = [jax.random.randint(jax.random.fold_in(key, axis), (), 0, dims[axis]) for axis in range(len(dims))]
    drawn = drawn.at[tuple(place)].set(least)
    longest = dims.index(max(dims))
    place[longest] = (place[longest] + 1) % dims[longest]
    return drawn.at[tuple(place)].set(largest)


def levels(own_key, dims, split, least, top_value):
    def one(position, blocks):
        heights = jax.random.uniform(jax.random.fold_in(jax.random.fold_in(own_key, 6), position), (blocks,), jnp.float32, least / len(split), top_value / len(split))
        return jnp.repeat(jnp.exp(heights), dims[position] // blocks).reshape((-1,) + (1,) * (len(dims) - position - 1))

    level = one(*split[0])
    for cut in split[1:]:
        level = level * one(*cut)
    return level


def gaussian(rng, dims, width, most, pieces=(), dtype=jnp.bfloat16):
    loudness = levels(rng, dims, pieces, -0.22, 0.18) if pieces else 1.0
    drawn = jax.random.normal(rng, dims, jnp.float32) * width * loudness
    return jnp.minimum(jnp.maximum(drawn, -most), most).astype(dtype)


def setup_inputs(seed: int = 0, part: int = 0) -> dict:
    key_list = jax.random.split(jax.random.key(seed), 7)
    own_keys = jax.random.split(jax.random.fold_in(key_list[6], part), 7)
    image = gaussian(own_keys[0], (3, HEIGHT, WIDTH), 1.0, 6.0, ((1, 16),), jnp.float32)
    grad_x = gaussian(own_keys[1], (3, HEIGHT, WIDTH), 1.0, 6.0, ((1, 16),))
    grad_y = gaussian(own_keys[2], (3, HEIGHT, WIDTH), 1.0, 6.0, ((1, 16),))
    classes = set_ends(jax.random.randint(own_keys[3], (HEIGHT, WIDTH), 0, 4), jax.random.fold_in(own_keys[3], 1), 0, 3).astype(jnp.int32)
    validity = set_ends((jax.random.randint(own_keys[4], (TILES_Y, TILES_X), 0, 4) < 3).astype(jnp.int32), jax.random.fold_in(own_keys[4], 1), 0, 1)
    owners = set_ends(jax.random.randint(own_keys[5], (TILES_Y, TILES_X, 2), 0, 2), jax.random.fold_in(own_keys[5], 1), 0, 1).astype(jnp.int32)
    return dict(image=image, grad_x=grad_x, grad_y=grad_y, classes=classes, validity=validity, owners=owners)


OMEGA = 0.8
SCREEN = 0.25


def blend_seams(horizontal, vertical, owners):
    vert_tiles = vertical.reshape(3, TILES_Y, TILE_ROWS, WIDTH)
    upper_mean = jnp.mean(vert_tiles[:, :-1, TILE_ROWS - 1 - BAND:TILE_ROWS - 1, :], axis=2)
    lower_mean = jnp.mean(vert_tiles[:, 1:, :BAND, :], axis=2)
    lower_owns = jnp.repeat(owners[:-1, :, 0], TILE_COLS, axis=1)[None] == 1
    vert_tiles = vert_tiles.at[:, :-1, TILE_ROWS - 1, :].set(jnp.where(lower_owns, lower_mean, upper_mean))
    horiz_tiles = horizontal.reshape(3, HEIGHT, TILES_X, TILE_COLS)
    left_mean = jnp.mean(horiz_tiles[:, :, :-1, TILE_COLS - 1 - BAND:TILE_COLS - 1], axis=3)
    right_mean = jnp.mean(horiz_tiles[:, :, 1:, :BAND], axis=3)
    right_owns = jnp.repeat(owners[:, :-1, 1], TILE_ROWS, axis=0)[None] == 1
    horiz_tiles = horiz_tiles.at[:, :, :-1, TILE_COLS - 1].set(jnp.where(right_owns, right_mean, left_mean))
    return horiz_tiles.reshape(3, HEIGHT, WIDTH), vert_tiles.reshape(3, HEIGHT, WIDTH)


def divergence(horiz_pad, vert_pad):
    horiz_here = horiz_pad[:, 1:, 1:-1]
    horiz_left = horiz_pad[:, 1:, :-2]
    horiz_above = horiz_pad[:, :-1, 1:-1]
    horiz_corner = horiz_pad[:, :-1, :-2]
    vert_here = vert_pad[:, 1:, 1:-1]
    vert_right = vert_pad[:, 1:, 2:]
    vert_left = vert_pad[:, 1:, :-2]
    vert_above = vert_pad[:, :-1, 1:-1]
    diagonal = horiz_here + vert_right - horiz_corner - vert_above + vert_left - horiz_left - vert_above + horiz_above
    return horiz_here - horiz_left + vert_here - vert_above + 0.5 * diagonal


def neighbours(padded):
    axial = padded[:, :-2, 1:-1] + padded[:, 2:, 1:-1] + padded[:, 1:-1, :-2] + padded[:, 1:-1, 2:]
    corner = padded[:, :-2, :-2] + padded[:, :-2, 2:] + padded[:, 2:, :-2] + padded[:, 2:, 2:]
    return axial + 0.5 * corner


def relax(row_padded, target, div_term, weights):
    current = row_padded[:, 1:-1, :]
    padded = jnp.pad(row_padded, ((0, 0), (0, 0), (1, 1)))
    return (1.0 - OMEGA) * current + OMEGA * (weights * target + neighbours(padded) - div_term) / (weights + 6.0)


def reference(image, grad_x, grad_y, classes, validity, owners):
    horizontal, vertical = blend_seams(grad_x.astype(jnp.float32), grad_y.astype(jnp.float32), owners)
    mean_vert = jnp.mean(vertical, axis=2)
    mean_image = jnp.mean(image, axis=2)
    level = jnp.cumsum(mean_vert, axis=1) - mean_vert - mean_image + mean_image[:, :1]
    target = image + level[:, :, None]
    cover = jnp.repeat(jnp.repeat(validity, TILE_ROWS, axis=0), TILE_COLS, axis=1).astype(jnp.float32)
    weights = cover * SCREEN * jnp.exp2(classes.astype(jnp.float32))
    edge = ((0, 0), (1, 0), (1, 1))
    div_term = divergence(jnp.pad(horizontal, edge), jnp.pad(vertical, edge))
    solution = target
    for sweep in range(SWEEPS):
        solution = relax(jnp.pad(solution, ((0, 0), (1, 1), (0, 0))), target, div_term, weights)
    return solution
```

```python
import jax
import jax.numpy as jnp
from jax import lax
from jax.sharding import PartitionSpec as P

TILE_ROWS = 1024
TILE_COLS = 1024
TILES_X = 4
BAND = 48
SWEEPS = 4
WIDTH = 4096


OMEGA = 0.8
SCREEN = 0.25


def passed_along(x, axis, by):
    devices = lax.axis_size(axis)
    pairs = [(i, i + by) for i in range(devices) if 0 <= i + by < devices]
    return lax.ppermute(x, axis, pairs)


def carried_in(x, axis, combine, identity):
    devices, position = (lax.axis_size(axis), lax.axis_index(axis))
    everything = jax.tree.map(lambda part: lax.all_gather(part, axis), x)
    start = jax.tree.map(
        lambda part, zero: jnp.broadcast_to(jnp.asarray(zero, part.dtype), part.shape), x, identity
    )

    def turn(k, before):
        reached = k < position
        new = combine(before, jax.tree.map(lambda part: part[k], everything))
        return jax.tree.map(lambda a, b: jnp.where(reached, a, b), new, before)

    return lax.fori_loop(0, devices, turn, start)


def with_halo(block, sides, width):
    for axis, dim in sides:
        count = lax.axis_size(axis)
        forward = [(i, i + 1) for i in range(count - 1)]
        backward = [(target, source) for source, target in forward]
        low = lax.ppermute(
            lax.slice_in_dim(block, block.shape[dim] - width, None, axis=dim), axis, forward
        )
        high = lax.ppermute(lax.slice_in_dim(block, 0, width, axis=dim), axis, backward)
        block = jnp.concatenate([low, block, high], axis=dim)
    return block


def divergence(horiz_pad, vert_pad):
    horiz_here = horiz_pad[:, 1:, 1:-1]
    horiz_left = horiz_pad[:, 1:, :-2]
    horiz_above = horiz_pad[:, :-1, 1:-1]
    horiz_corner = horiz_pad[:, :-1, :-2]
    vert_here = vert_pad[:, 1:, 1:-1]
    vert_right = vert_pad[:, 1:, 2:]
    vert_left = vert_pad[:, 1:, :-2]
    vert_above = vert_pad[:, :-1, 1:-1]
    diagonal = (
        horiz_here
        + vert_right
        - horiz_corner
        - vert_above
        + vert_left
        - horiz_left
        - vert_above
        + horiz_above
    )
    return horiz_here - horiz_left + vert_here - vert_above + 0.5 * diagonal


def neighbours(padded):
    axial = padded[:, :-2, 1:-1] + padded[:, 2:, 1:-1] + padded[:, 1:-1, :-2] + padded[:, 1:-1, 2:]
    corner = padded[:, :-2, :-2] + padded[:, :-2, 2:] + padded[:, 2:, :-2] + padded[:, 2:, 2:]
    return axial + 0.5 * corner


def relax(row_padded, target, div_term, weights):
    current = row_padded[:, 1:-1, :]
    padded = jnp.pad(row_padded, ((0, 0), (0, 0), (1, 1)))
    return (1.0 - OMEGA) * current + OMEGA * (weights * target + neighbours(padded) - div_term) / (
        weights + 6.0
    )


def join_prefix(earlier, later):
    return (
        earlier[0] + later[0],
        jnp.where(earlier[2] > 0, earlier[1], later[1]),
        jnp.maximum(earlier[2], later[2]),
    )


def per_device(image, grad_x, grad_y, classes, validity, owners):
    band_rows = image.shape[1]
    devices = lax.axis_size("row")
    position = lax.axis_index("row")
    first_row = position * band_rows
    horizontal = grad_x.astype(jnp.float32)
    vertical = grad_y.astype(jnp.float32)
    tile_row = first_row // TILE_ROWS
    own_row = lax.dynamic_index_in_dim(owners, tile_row, 0, keepdims=False)
    lower_mean = passed_along(
        jnp.mean(vertical[:, :BAND, :], axis=1).astype(jnp.bfloat16), "row", -1
    ).astype(jnp.float32)
    upper_mean = jnp.mean(vertical[:, band_rows - 1 - BAND : band_rows - 1, :], axis=1)
    lower_owns = jnp.repeat(own_row[:, 0], TILE_COLS, total_repeat_length=WIDTH)[None] == 1
    at_seam = ((first_row + band_rows) % TILE_ROWS == 0) & (position < devices - 1)
    last_row = jnp.where(at_seam, jnp.where(lower_owns, lower_mean, upper_mean), vertical[:, -1, :])
    vertical = vertical.at[:, -1, :].set(last_row)
    horiz_tiles = horizontal.reshape(3, band_rows, TILES_X, TILE_COLS)
    left_mean = jnp.mean(horiz_tiles[:, :, :-1, TILE_COLS - 1 - BAND : TILE_COLS - 1], axis=3)
    right_mean = jnp.mean(horiz_tiles[:, :, 1:, :BAND], axis=3)
    right_owns = (own_row[:-1, 1] == 1)[None, None, :]
    horiz_tiles = horiz_tiles.at[:, :, :-1, TILE_COLS - 1].set(
        jnp.where(right_owns, right_mean, left_mean)
    )
    horizontal = horiz_tiles.reshape(3, band_rows, WIDTH)
    above_horiz, above_vert = (
        passed_along(horizontal[:, -1:, :].astype(jnp.bfloat16), "row", 1).astype(jnp.float32),
        passed_along(vertical[:, -1:, :].astype(jnp.bfloat16), "row", 1).astype(jnp.float32),
    )
    column_pad = ((0, 0), (0, 0), (1, 1))
    div_term = divergence(
        jnp.pad(jnp.concatenate([above_horiz, horizontal], axis=1), column_pad),
        jnp.pad(jnp.concatenate([above_vert, vertical], axis=1), column_pad),
    )
    mean_vert = jnp.mean(vertical, axis=2)
    mean_image = jnp.mean(image, axis=2)
    above = jnp.arange(band_rows)
    strictly = (above[None, :] < above[:, None]).astype(jnp.float32)
    running = jnp.sum(strictly[None] * mean_vert[:, None, :], axis=2)
    totals = jnp.sum(mean_vert, axis=1)
    leading = mean_image[:, 0]
    empty_three = jnp.zeros((3,), jnp.float32)
    before, prior_first, prior_seen = carried_in(
        (totals, leading, jnp.ones((1,), jnp.float32)),
        "row",
        join_prefix,
        (empty_three, empty_three, jnp.zeros((1,), jnp.float32)),
    )
    window_first = jnp.where(prior_seen > 0, prior_first, leading)
    level = before[:, None] + running - mean_image + window_first[:, None]
    target = image + level[:, :, None]
    cover = jnp.repeat(
        lax.dynamic_index_in_dim(validity, tile_row, 0, keepdims=False),
        TILE_COLS,
        total_repeat_length=WIDTH,
    ).astype(jnp.float32)
    weights = cover[None, :] * SCREEN * jnp.exp2(classes.astype(jnp.float32))
    solution = target
    for sweep in range(SWEEPS):
        row_padded = with_halo(solution, (("row", 1),), 1)
        solution = relax(row_padded, target, div_term, weights)
    return solution


def solution(mesh):
    in_specs = (
        P(None, ("win", "row"), None),
        P(None, ("win", "row"), None),
        P(None, ("win", "row"), None),
        P(("win", "row"), None),
        P("win", None),
        P("win", None, None),
    )
    out_specs = P(None, ("win", "row"), None)
    return jax.shard_map(
        per_device, mesh=mesh, in_specs=in_specs, out_specs=out_specs, check_vma=False
    )
```

```python
import functools

import jax
import jax.numpy as jnp
from jax import lax
from jax.experimental import pallas as pl
from jax.experimental.pallas import tpu as pltpu
from jax.sharding import PartitionSpec as P

TILE_ROWS = 1024
TILE_COLS = 1024
BAND = 48
SWEEPS = 4
OMEGA = 0.8
SCREEN = 0.25
LANES = 128
SUB = 8
PAD = 8
MESH = pl.DeviceIdType.MESH


def kernel(
    n, image, grad_x, grad_y, classes, validity, owners, out,
    s, a_term, b_term, gxf, gyf, sums, level, tot, gathered, band_out, band_in,
    halo_send, halo_recv, grad_send, grad_recv, tot_send, tot_recv, band_sems,
):
    channels, rows, width = image.shape
    blocks, tiles = width // LANES, rows // SUB
    per_tile = TILE_COLS // LANES
    seams_below = validity.shape[0] > 1
    pos = lax.axis_index("row")
    win = lax.axis_index("win")
    tile_row = pos * rows // TILE_ROWS
    lane = lax.broadcasted_iota(jnp.int32, (SUB, LANES), 1)
    lane16 = lax.broadcasted_iota(jnp.int32, (2 * SUB, LANES), 1)
    first_lane, last_lane = lane == 0, lane == LANES - 1
    zero = jnp.zeros((SUB, LANES), jnp.float32)
    has_above, has_below = pos > 0, pos < n - 1

    barrier = pltpu.get_barrier_semaphore()

    def greet(j, carry):
        @pl.when((j < pos) | (j == pos + 1))
        def _():
            pl.semaphore_signal(barrier, inc=1, device_id=(win, j), device_id_type=MESH)
        return carry

    lax.fori_loop(0, n, greet, 0)

    def remote(src, dst, send, recv, to):
        return pltpu.make_async_remote_copy(
            src_ref=src, dst_ref=dst, send_sem=send, recv_sem=recv,
            device_id=(win, to), device_id_type=MESH,
        )

    def row_of(ref, row):
        return ref.at[:, :, pl.ds(row, 1), :]

    def gy_pass(j, carry):
        k, at = j // (tiles // 2), (j % (tiles // 2)) * 2 * SUB
        total = [None, None]
        for c in range(blocks):
            v = grad_y[k, pl.ds(at, 2 * SUB), c * LANES:(c + 1) * LANES].astype(jnp.float32)
            gyf[k, c, pl.ds(PAD + at, 2 * SUB), :] = v
            total[c % 2] = v if total[c % 2] is None else total[c % 2] + v
        sums[0, k, pl.ds(at, 2 * SUB), :] = total[0] + total[1]
        return carry

    lax.fori_loop(0, channels * tiles // 2, gy_pass, 0)

    def gx_pass(j, carry):
        k, at = j // (tiles // 2), (j % (tiles // 2)) * 2 * SUB
        for c in range(blocks):
            v = grad_x[k, pl.ds(at, 2 * SUB), c * LANES:(c + 1) * LANES].astype(jnp.float32)
            if (c + 1) % per_tile == 0 and c + 1 < blocks:
                after = grad_x[k, pl.ds(at, 2 * SUB), (c + 1) * LANES:(c + 2) * LANES].astype(jnp.float32)
                inside = (lane16 >= LANES - 1 - BAND) & (lane16 < LANES - 1)
                left = jnp.sum(jnp.where(inside, v, 0.0), axis=1, keepdims=True)
                right = jnp.sum(jnp.where(lane16 < BAND, after, 0.0), axis=1, keepdims=True)
                owns = owners[tile_row, c // per_tile, 1] == 1
                mean = jnp.where(owns, right, left) * (1.0 / BAND)
                v = jnp.where(lane16 == LANES - 1, mean, v)
            gxf[k, c, pl.ds(PAD + at, 2 * SUB), :] = v
        return carry

    lax.fori_loop(0, channels * tiles // 2, gx_pass, 0)

    pl.semaphore_wait(barrier, n - 1 - pos + jnp.where(has_above, 1, 0))

    if seams_below:
        def band_pass(j, carry):
            k, c = j // blocks, j % blocks
            mean = jnp.sum(gyf[k, c, PAD:PAD + BAND, :], axis=0, keepdims=True) * (1.0 / BAND)
            band_out[k, c] = jnp.broadcast_to(mean, (SUB, LANES))
            return carry

        lax.fori_loop(0, channels * blocks, band_pass, 0)
        band = remote(row_of(band_out, 0), row_of(band_in, 0), band_sems.at[0], band_sems.at[1], pos - 1)

        @pl.when(has_above)
        def _():
            band.start()

        @pl.when(has_below)
        def _():
            band.wait_recv()

        @pl.when(has_above)
        def _():
            band.wait_send()

        at_seam = has_below & ((pos + 1) * rows % TILE_ROWS == 0)

        @pl.when(at_seam)
        def _():
            last = PAD + rows - 1
            for k in range(channels):
                total = jnp.zeros((1, LANES), jnp.float32)
                for c in range(blocks):
                    upper = jnp.sum(gyf[k, c, last - BAND:last, :], axis=0, keepdims=True) * (1.0 / BAND)
                    owns = owners[tile_row, c // per_tile, 0] == 1
                    new = jnp.where(owns, band_in[k, c, 0:1, :], upper)
                    gyf[k, c, last:last + 1, :] = new
                    total = total + new
                sums[0, k, rows - 1:rows, :] = total

    grads = [
        remote(row_of(g, PAD + rows - 1), row_of(g, PAD - 1), grad_send.at[q], grad_recv.at[q], pos + 1)
        for q, g in enumerate((gxf, gyf))
    ]

    @pl.when(has_below)
    def _():
        for copy in grads:
            copy.start()

    tot[...] = zero
    for k in range(channels):
        first = image[k, 0:SUB, 0:LANES]
        for c in range(1, blocks):
            first = first + image[k, 0:SUB, c * LANES:(c + 1) * LANES]
        mean = jnp.sum(first, axis=1, keepdims=True) * (1.0 / width)
        tot[channels + k:channels + k + 1, :] = jnp.broadcast_to(mean[0:1], (1, LANES))
        my = jnp.sum(sums[0, k], axis=1, keepdims=True) * (1.0 / width)
        sums[0, k] = jnp.broadcast_to(my, (rows, LANES))
        tot[k:k + 1, :] = jnp.broadcast_to(jnp.sum(my, axis=0, keepdims=True), (1, LANES))

    def tell(j, carry):
        @pl.when(j > pos)
        def _():
            remote(tot, gathered.at[pos], tot_send.at[j], tot_recv.at[pos], j).start()
        return carry

    lax.fori_loop(0, n, tell, 0)

    @pl.when(jnp.logical_not(has_above))
    def _():
        for k in range(channels):
            for c in range(blocks):
                gxf[k, c, PAD - 1:PAD, :] = zero[:1]
                gyf[k, c, PAD - 1:PAD, :] = zero[:1]
                for t in range(SWEEPS):
                    s[t, k, c, PAD - 1:PAD, :] = zero[:1]

    @pl.when(jnp.logical_not(has_below))
    def _():
        for k in range(channels):
            for c in range(blocks):
                for t in range(SWEEPS):
                    s[t, k, c, PAD + rows:PAD + rows + 1, :] = zero[:1]

    def image_pass(j, carry):
        k, at = j // tiles, (j % tiles) * SUB
        total = [None, None]
        for c in range(blocks):
            v = image[k, pl.ds(at, SUB), c * LANES:(c + 1) * LANES]
            total[c % 2] = v if total[c % 2] is None else total[c % 2] + v
        sums[1, k, pl.ds(at, SUB), :] = total[0] + total[1]
        return carry

    lax.fori_loop(0, channels * tiles, image_pass, 0)

    def weight_pass(i, carry):
        at = i * SUB
        for c in range(blocks):
            power = (1 << classes[pl.ds(at, SUB), c * LANES:(c + 1) * LANES]).astype(jnp.float32)
            cover = validity[tile_row, c // per_tile].astype(jnp.float32) * SCREEN
            b_term[c, pl.ds(at, SUB), :] = OMEGA / (cover * power + 6.0)
        return carry

    lax.fori_loop(0, tiles, weight_pass, 0)

    def div_tile(k, i):
        at = i * SUB
        state = []

        def load(c):
            x0, xm = gxf[k, c, pl.ds(PAD + at, SUB), :], gxf[k, c, pl.ds(PAD - 1 + at, SUB), :]
            y0, ym = gyf[k, c, pl.ds(PAD + at, SUB), :], gyf[k, c, pl.ds(PAD - 1 + at, SUB), :]
            x = 1.5 * x0 + 0.5 * xm
            y = 0.5 * y0
            return x + y0 - 2.0 * ym, pltpu.roll(y - x, 1, 1), pltpu.roll(y, LANES - 1, 1)

        before, here = zero, load(0)
        for c in range(blocks):
            after = load(c + 1) if c + 1 < blocks else (None, None, zero)
            base, left, right = here
            moved = jnp.where(first_lane, before, left) + jnp.where(last_lane, after[2], right)
            a_term[k, c, pl.ds(at, SUB), :] = b_term[c, pl.ds(at, SUB), :] * (base + moved)
            before, here = left, after

    def div_loop(j, carry):
        div_tile(j // (tiles - 1), 1 + j % (tiles - 1))
        return carry

    lax.fori_loop(0, channels * (tiles - 1), div_loop, 0)

    @pl.when(has_above)
    def _():
        for copy in grads:
            copy.wait_recv()

    def div_first(k, carry):
        div_tile(k, 0)
        return carry

    lax.fori_loop(0, channels, div_first, 0)

    down = lax.broadcasted_iota(jnp.int32, (rows, rows), 0)
    across = lax.broadcasted_iota(jnp.int32, (rows, rows), 1)
    strictly = (across < down).astype(jnp.float32)
    for k in range(channels):
        running = jnp.dot(
            strictly, sums[0, k], precision=lax.Precision.HIGHEST, preferred_element_type=jnp.float32
        )
        mf = jnp.sum(sums[1, k], axis=1, keepdims=True) * (1.0 / width)
        level[k] = running - mf

    gathered[pos] = tot[...]

    def hear(j, carry):
        @pl.when(j < pos)
        def _():
            remote(tot, gathered.at[j], tot_send.at[j], tot_recv.at[j], j).wait_recv()
        return carry

    lax.fori_loop(0, n, hear, 0)
    before = lax.fori_loop(0, pos, lambda j, total: total + gathered[j], zero)
    leading = gathered[0]
    for k in range(channels):
        level[k] = level[k] + (before[k:k + 1, :] + leading[channels + k:channels + k + 1, :])

    def start_tile(k, i):
        at = i * SUB
        up = level[k, pl.ds(at, SUB), :]
        for c in range(blocks):
            target = image[k, pl.ds(at, SUB), c * LANES:(c + 1) * LANES] + up
            s[0, k, c, pl.ds(PAD + at, SUB), :] = target
            rest = OMEGA - 6.0 * b_term[c, pl.ds(at, SUB), :]
            a_term[k, c, pl.ds(at, SUB), :] = rest * target - a_term[k, c, pl.ds(at, SUB), :]

    def sweep_tile(t, k, i):
        at = i * SUB

        def load(c):
            mid = s[t, k, c, pl.ds(PAD + at, SUB), :]
            v = s[t, k, c, pl.ds(PAD - 1 + at, SUB), :] + s[t, k, c, pl.ds(PAD + 1 + at, SUB), :]
            q = mid + 0.5 * v
            return mid, v, pltpu.roll(q, 1, 1), pltpu.roll(q, LANES - 1, 1)

        before, here = zero, load(0)
        for c in range(blocks):
            after = load(c + 1) if c + 1 < blocks else (None, None, None, zero)
            mid, v, left, right = here
            around = v + jnp.where(first_lane, before, left) + jnp.where(last_lane, after[3], right)
            new = (1.0 - OMEGA) * mid + (
                a_term[k, c, pl.ds(at, SUB), :] + b_term[c, pl.ds(at, SUB), :] * around
            )
            if t + 1 < SWEEPS:
                s[t + 1, k, c, pl.ds(PAD + at, SUB), :] = new
            else:
                out[k, pl.ds(at, SUB), c * LANES:(c + 1) * LANES] = new
            before, here = left, after

    def halo(t):
        up = remote(row_of(s.at[t], PAD), row_of(s.at[t], PAD + rows), halo_send.at[t, 0], halo_recv.at[t, 0], pos - 1)
        dn = remote(row_of(s.at[t], PAD + rows - 1), row_of(s.at[t], PAD - 1), halo_send.at[t, 1], halo_recv.at[t, 1], pos + 1)
        return up, dn

    def rim_then_inner(work, t):
        def rim(j, carry):
            work(j // 2, (j % 2) * (tiles - 1))
            return carry

        def inner(j, carry):
            work(j // (tiles - 2), 1 + j % (tiles - 2))
            return carry

        lax.fori_loop(0, channels * 2, rim, 0)
        if t < SWEEPS:
            up, dn = halo(t)

            @pl.when(has_above)
            def _():
                up.start()

            @pl.when(has_below)
            def _():
                dn.start()

        lax.fori_loop(0, channels * (tiles - 2), inner, 0)
        if t < SWEEPS:
            @pl.when(has_below)
            def _():
                up.wait_recv()

            @pl.when(has_above)
            def _():
                dn.wait_recv()

    rim_then_inner(start_tile, 0)
    for t in range(SWEEPS):
        rim_then_inner(functools.partial(sweep_tile, t), t + 1)

    for t in range(SWEEPS):
        up, dn = halo(t)

        @pl.when(has_above)
        def _():
            up.wait_send()

        @pl.when(has_below)
        def _():
            dn.wait_send()

    @pl.when(has_below)
    def _():
        for copy in grads:
            copy.wait_send()

    def sent(j, carry):
        @pl.when(j > pos)
        def _():
            remote(tot, gathered.at[pos], tot_send.at[j], tot_recv.at[pos], j).wait_send()
        return carry

    lax.fori_loop(0, n, sent, 0)


def per_device(image, grad_x, grad_y, classes, validity, owners):
    n = lax.axis_size("row")
    channels, rows, width = image.shape
    blocks = width // LANES
    vmem, smem = pl.BlockSpec(memory_space=pltpu.VMEM), pl.BlockSpec(memory_space=pltpu.SMEM)
    f32 = jnp.float32
    band_rows = SUB if validity.shape[0] > 1 else 1
    band_blocks = blocks if validity.shape[0] > 1 else 1
    return pl.pallas_call(
        functools.partial(kernel, n),
        out_shape=jax.ShapeDtypeStruct(image.shape, f32),
        in_specs=[vmem] * 4 + [smem] * 2,
        out_specs=vmem,
        scratch_shapes=[
            pltpu.VMEM((SWEEPS, channels, blocks, PAD + rows + SUB, LANES), f32),
            pltpu.VMEM((channels, blocks, rows, LANES), f32),
            pltpu.VMEM((blocks, rows, LANES), f32),
            pltpu.VMEM((channels, blocks, PAD + rows, LANES), f32),
            pltpu.VMEM((channels, blocks, PAD + rows, LANES), f32),
            pltpu.VMEM((2, channels, rows, LANES), f32),
            pltpu.VMEM((channels, rows, LANES), f32),
            pltpu.VMEM((SUB, LANES), f32),
            pltpu.VMEM((n, SUB, LANES), f32),
            pltpu.VMEM((channels, band_blocks, band_rows, LANES), f32),
            pltpu.VMEM((channels, band_blocks, band_rows, LANES), f32),
            pltpu.SemaphoreType.DMA((SWEEPS, 2)),
            pltpu.SemaphoreType.DMA((SWEEPS, 2)),
            pltpu.SemaphoreType.DMA((2,)),
            pltpu.SemaphoreType.DMA((2,)),
            pltpu.SemaphoreType.DMA((n,)),
            pltpu.SemaphoreType.DMA((n,)),
            pltpu.SemaphoreType.DMA((2,)),
        ],
        compiler_params=pltpu.CompilerParams(
            collective_id=0, has_side_effects=True, vmem_limit_bytes=56 * 2**20
        ),
    )(image, grad_x, grad_y, classes, validity, owners)


def solution(mesh):
    in_specs = (
        P(None, ("win", "row"), None),
        P(None, ("win", "row"), None),
        P(None, ("win", "row"), None),
        P(("win", "row"), None),
        P("win", None),
        P("win", None, None),
    )
    out_specs = P(None, ("win", "row"), None)
    return jax.shard_map(
        per_device, mesh=mesh, in_specs=in_specs, out_specs=out_specs, check_vma=False
    )
```

```python
import functools

import jax
import jax.numpy as jnp
from jax import lax
from jax.experimental import pallas as pl
from jax.experimental.pallas import tpu as pltpu
from jax.sharding import PartitionSpec as P

TILE_ROWS = 1024
TILE_COLS = 1024
BAND = 48
SWEEPS = 4
OMEGA = 0.8
SCREEN = 0.25
LANES = 128
SUB = 8
PAD = 8
MESH = pl.DeviceIdType.MESH


def kernel(
    n, image_in, gx_in, gy_in, classes_in, validity, owners, out,
    image, grad_x, grad_y, classes, s0, s1, s2, s3, d_term, a_term, b_term, gxf, gyf, sums, level, tot, gathered, band_out, band_in,
    halo_send, halo_recv, grad_send, grad_recv, tot_send, tot_recv, band_sems, in_sems,
):
    channels, rows, width = image_in.shape
    blocks, tiles = width // LANES, rows // SUB
    per_tile = TILE_COLS // LANES
    seams_below = validity.shape[0] > 1
    pos = lax.axis_index("row")
    win = lax.axis_index("win")
    tile_row = pos * rows // TILE_ROWS
    lane = lax.broadcasted_iota(jnp.int32, (SUB, LANES), 1)
    lane16 = lax.broadcasted_iota(jnp.int32, (2 * SUB, LANES), 1)
    first_lane, last_lane = lane == 0, lane == LANES - 1
    zero = jnp.zeros((SUB, LANES), jnp.float32)
    has_above, has_below = pos > 0, pos < n - 1

    iterates = (s0, s1, s2, s3)
    fetch_gy, fetch_gx, fetch_image, fetch_classes = (
        pltpu.make_async_copy(src, dst, in_sems.at[q])
        for q, (src, dst) in enumerate(
            ((gy_in, grad_y), (gx_in, grad_x), (image_in, image), (classes_in, classes))
        )
    )
    for fetch in (fetch_gy, fetch_gx, fetch_image, fetch_classes):
        fetch.start()

    barrier = pltpu.get_barrier_semaphore()

    def greet(j, carry):
        @pl.when((j < pos) | (j == pos + 1))
        def _():
            pl.semaphore_signal(barrier, inc=1, device_id=(win, j), device_id_type=MESH)
        return carry

    lax.fori_loop(0, n, greet, 0)

    def remote(src, dst, send, recv, to):
        return pltpu.make_async_remote_copy(
            src_ref=src, dst_ref=dst, send_sem=send, recv_sem=recv,
            device_id=(win, to), device_id_type=MESH,
        )

    def row_of(ref, row):
        return ref.at[:, :, pl.ds(row, 1), :]

    def gy_pass(j, carry):
        k, at = j // (tiles // 2), (j % (tiles // 2)) * 2 * SUB
        total = [None, None]
        for c in range(blocks):
            v = grad_y[k, pl.ds(at, 2 * SUB), c * LANES:(c + 1) * LANES].astype(jnp.float32)
            gyf[k, c, pl.ds(PAD + at, 2 * SUB), :] = v
            total[c % 2] = v if total[c % 2] is None else total[c % 2] + v
        sums[0, k, pl.ds(at, 2 * SUB), :] = total[0] + total[1]
        return carry

    fetch_gy.wait()
    lax.fori_loop(0, channels * tiles // 2, gy_pass, 0)

    def gx_pass(j, carry):
        k, at = j // (tiles // 2), (j % (tiles // 2)) * 2 * SUB
        for c in range(blocks):
            v = grad_x[k, pl.ds(at, 2 * SUB), c * LANES:(c + 1) * LANES].astype(jnp.float32)
            if (c + 1) % per_tile == 0 and c + 1 < blocks:
                after = grad_x[k, pl.ds(at, 2 * SUB), (c + 1) * LANES:(c + 2) * LANES].astype(jnp.float32)
                inside = (lane16 >= LANES - 1 - BAND) & (lane16 < LANES - 1)
                left = jnp.sum(jnp.where(inside, v, 0.0), axis=1, keepdims=True)
                right = jnp.sum(jnp.where(lane16 < BAND, after, 0.0), axis=1, keepdims=True)
                owns = owners[tile_row, 1, c // per_tile] == 1
                mean = jnp.where(owns, right, left) * (1.0 / BAND)
                v = jnp.where(lane16 == LANES - 1, mean, v)
            gxf[k, c, pl.ds(PAD + at, 2 * SUB), :] = v
        return carry

    fetch_gx.wait()
    lax.fori_loop(0, channels * tiles // 2, gx_pass, 0)

    pl.semaphore_wait(barrier, n - 1 - pos + jnp.where(has_above, 1, 0))

    if seams_below:
        def band_pass(j, carry):
            k, c = j // blocks, j % blocks
            mean = jnp.sum(gyf[k, c, PAD:PAD + BAND, :], axis=0, keepdims=True) * (1.0 / BAND)
            band_out[k, c] = jnp.broadcast_to(mean, (SUB, LANES))
            return carry

        lax.fori_loop(0, channels * blocks, band_pass, 0)
        band = remote(row_of(band_out, 0), row_of(band_in, 0), band_sems.at[0], band_sems.at[1], pos - 1)

        @pl.when(has_above)
        def _():
            band.start()

        @pl.when(has_below)
        def _():
            band.wait_recv()

        @pl.when(has_above)
        def _():
            band.wait_send()

        at_seam = has_below & ((pos + 1) * rows % TILE_ROWS == 0)

        @pl.when(at_seam)
        def _():
            last = PAD + rows - 1
            for k in range(channels):
                total = jnp.zeros((1, LANES), jnp.float32)
                for c in range(blocks):
                    upper = jnp.sum(gyf[k, c, last - BAND:last, :], axis=0, keepdims=True) * (1.0 / BAND)
                    owns = owners[tile_row, 0, c // per_tile] == 1
                    new = jnp.where(owns, band_in[k, c, 0:1, :], upper)
                    gyf[k, c, last:last + 1, :] = new
                    total = total + new
                sums[0, k, rows - 1:rows, :] = total

    grads = [
        remote(row_of(g, PAD + rows - 1), row_of(g, PAD - 1), grad_send.at[q], grad_recv.at[q], pos + 1)
        for q, g in enumerate((gxf, gyf))
    ]

    @pl.when(has_below)
    def _():
        for copy in grads:
            copy.start()

    fetch_image.wait()
    tot[...] = zero
    for k in range(channels):
        first = image[k, 0:SUB, 0:LANES]
        for c in range(1, blocks):
            first = first + image[k, 0:SUB, c * LANES:(c + 1) * LANES]
        mean = jnp.sum(first, axis=1, keepdims=True) * (1.0 / width)
        tot[channels + k:channels + k + 1, :] = jnp.broadcast_to(mean[0:1], (1, LANES))
        my = jnp.sum(sums[0, k], axis=1, keepdims=True) * (1.0 / width)
        sums[0, k] = jnp.broadcast_to(my, (rows, LANES))
        tot[k:k + 1, :] = jnp.broadcast_to(jnp.sum(my, axis=0, keepdims=True), (1, LANES))

    def tell(j, carry):
        @pl.when(j > pos)
        def _():
            remote(tot, gathered.at[pos], tot_send.at[j], tot_recv.at[pos], j).start()
        return carry

    lax.fori_loop(0, n, tell, 0)

    @pl.when(jnp.logical_not(has_above))
    def _():
        for k in range(channels):
            for c in range(blocks):
                gxf[k, c, PAD - 1:PAD, :] = zero[:1]
                gyf[k, c, PAD - 1:PAD, :] = zero[:1]
                for t in range(SWEEPS):
                    iterates[t][k, c, PAD - 1:PAD, :] = zero[:1]

    @pl.when(jnp.logical_not(has_below))
    def _():
        for k in range(channels):
            for c in range(blocks):
                for t in range(SWEEPS):
                    iterates[t][k, c, PAD + rows:PAD + rows + 1, :] = zero[:1]

    def image_pass(j, carry):
        k, at = j // tiles, (j % tiles) * SUB
        total = [None, None]
        for c in range(blocks):
            v = image[k, pl.ds(at, SUB), c * LANES:(c + 1) * LANES]
            total[c % 2] = v if total[c % 2] is None else total[c % 2] + v
        sums[1, k, pl.ds(at, SUB), :] = total[0] + total[1]
        return carry

    lax.fori_loop(0, channels * tiles, image_pass, 0)

    def weight_pass(i, carry):
        at = i * SUB
        for c in range(blocks):
            power = (1 << classes[pl.ds(at, SUB), c * LANES:(c + 1) * LANES]).astype(jnp.float32)
            cover = validity[tile_row, c // per_tile].astype(jnp.float32) * SCREEN
            b_term[c, pl.ds(at, SUB), :] = OMEGA / (cover * power + 6.0)
        return carry

    fetch_classes.wait()
    lax.fori_loop(0, tiles, weight_pass, 0)

    def div_tile(k, i):
        at = i * SUB
        state = []

        def load(c):
            x0, xm = gxf[k, c, pl.ds(PAD + at, SUB), :], gxf[k, c, pl.ds(PAD - 1 + at, SUB), :]
            y0, ym = gyf[k, c, pl.ds(PAD + at, SUB), :], gyf[k, c, pl.ds(PAD - 1 + at, SUB), :]
            x = 1.5 * x0 + 0.5 * xm
            y = 0.5 * y0
            return x + y0 - 2.0 * ym, pltpu.roll(y - x, 1, 1), pltpu.roll(y, LANES - 1, 1)

        before, here = zero, load(0)
        for c in range(blocks):
            after = load(c + 1) if c + 1 < blocks else (None, None, zero)
            base, left, right = here
            moved = jnp.where(first_lane, before, left) + jnp.where(last_lane, after[2], right)
            d_term[k, c, pl.ds(at, SUB), :] = b_term[c, pl.ds(at, SUB), :] * (base + moved)
            before, here = left, after

    def div_loop(j, carry):
        div_tile(j // (tiles - 1), 1 + j % (tiles - 1))
        return carry

    lax.fori_loop(0, channels * (tiles - 1), div_loop, 0)

    @pl.when(has_above)
    def _():
        for copy in grads:
            copy.wait_recv()

    def div_first(k, carry):
        div_tile(k, 0)
        return carry

    lax.fori_loop(0, channels, div_first, 0)

    down = lax.broadcasted_iota(jnp.int32, (rows, rows), 0)
    across = lax.broadcasted_iota(jnp.int32, (rows, rows), 1)
    strictly = (across < down).astype(jnp.float32)
    for k in range(channels):
        running = jnp.dot(
            strictly, sums[0, k], precision=lax.Precision.HIGHEST, preferred_element_type=jnp.float32
        )
        mf = jnp.sum(sums[1, k], axis=1, keepdims=True) * (1.0 / width)
        level[k] = running - mf

    gathered[pos] = tot[...]

    def hear(j, carry):
        @pl.when(j < pos)
        def _():
            remote(tot, gathered.at[j], tot_send.at[j], tot_recv.at[j], j).wait_recv()
        return carry

    lax.fori_loop(0, n, hear, 0)
    before = lax.fori_loop(0, pos, lambda j, total: total + gathered[j], zero)
    leading = gathered[0]
    for k in range(channels):
        level[k] = level[k] + (before[k:k + 1, :] + leading[channels + k:channels + k + 1, :])

    def start_tile(k, i):
        at = i * SUB
        up = level[k, pl.ds(at, SUB), :]
        for c in range(blocks):
            target = image[k, pl.ds(at, SUB), c * LANES:(c + 1) * LANES] + up
            s0[k, c, pl.ds(PAD + at, SUB), :] = target
            rest = OMEGA - 6.0 * b_term[c, pl.ds(at, SUB), :]
            a_term[k, c, pl.ds(at, SUB), :] = rest * target - d_term[k, c, pl.ds(at, SUB), :]

    def sweep_tile(t, k, i):
        at = i * SUB

        def load(c):
            mid = iterates[t][k, c, pl.ds(PAD + at, SUB), :]
            v = iterates[t][k, c, pl.ds(PAD - 1 + at, SUB), :] + iterates[t][k, c, pl.ds(PAD + 1 + at, SUB), :]
            q = mid + 0.5 * v
            return mid, v, pltpu.roll(q, 1, 1), pltpu.roll(q, LANES - 1, 1)

        before, here = zero, load(0)
        for c in range(blocks):
            after = load(c + 1) if c + 1 < blocks else (None, None, None, zero)
            mid, v, left, right = here
            around = v + jnp.where(first_lane, before, left) + jnp.where(last_lane, after[3], right)
            new = (1.0 - OMEGA) * mid + (
                a_term[k, c, pl.ds(at, SUB), :] + b_term[c, pl.ds(at, SUB), :] * around
            )
            if t + 1 < SWEEPS:
                iterates[t + 1][k, c, pl.ds(PAD + at, SUB), :] = new
            else:
                out[k, pl.ds(at, SUB), c * LANES:(c + 1) * LANES] = new
            before, here = left, after

    def halo(t):
        up = remote(row_of(iterates[t], PAD), row_of(iterates[t], PAD + rows), halo_send.at[t, 0], halo_recv.at[t, 0], pos - 1)
        dn = remote(row_of(iterates[t], PAD + rows - 1), row_of(iterates[t], PAD - 1), halo_send.at[t, 1], halo_recv.at[t, 1], pos + 1)
        return up, dn

    def rim_then_inner(work, t):
        def rim(j, carry):
            work(j // 2, (j % 2) * (tiles - 1))
            return carry

        def inner(j, carry):
            work(j // (tiles - 2), 1 + j % (tiles - 2))
            return carry

        lax.fori_loop(0, channels * 2, rim, 0)
        if t < SWEEPS:
            up, dn = halo(t)

            @pl.when(has_above)
            def _():
                up.start()

            @pl.when(has_below)
            def _():
                dn.start()

        lax.fori_loop(0, channels * (tiles - 2), inner, 0)
        if t < SWEEPS:
            @pl.when(has_below)
            def _():
                up.wait_recv()

            @pl.when(has_above)
            def _():
                dn.wait_recv()

    rim_then_inner(start_tile, 0)
    for t in range(SWEEPS):
        rim_then_inner(functools.partial(sweep_tile, t), t + 1)

    for t in range(SWEEPS):
        up, dn = halo(t)

        @pl.when(has_above)
        def _():
            up.wait_send()

        @pl.when(has_below)
        def _():
            dn.wait_send()

    @pl.when(has_below)
    def _():
        for copy in grads:
            copy.wait_send()

    def sent(j, carry):
        @pl.when(j > pos)
        def _():
            remote(tot, gathered.at[pos], tot_send.at[j], tot_recv.at[pos], j).wait_send()
        return carry

    lax.fori_loop(0, n, sent, 0)


def per_device(image, grad_x, grad_y, classes, validity, owners):
    n = lax.axis_size("row")
    channels, rows, width = image.shape
    blocks = width // LANES
    vmem, smem = pl.BlockSpec(memory_space=pltpu.VMEM), pl.BlockSpec(memory_space=pltpu.SMEM)
    f32 = jnp.float32
    band_rows = SUB if validity.shape[0] > 1 else 1
    band_blocks = blocks if validity.shape[0] > 1 else 1
    return pl.pallas_call(
        functools.partial(kernel, n),
        out_shape=pltpu.VMEM(image.shape, f32),
        in_specs=[pl.BlockSpec(memory_space=pl.ANY)] * 4 + [smem] * 2,
        out_specs=vmem,
        scratch_shapes=[
            pltpu.VMEM(image.shape, image.dtype),
            pltpu.VMEM(grad_x.shape, grad_x.dtype),
            pltpu.VMEM(grad_y.shape, grad_y.dtype),
            pltpu.VMEM(classes.shape, classes.dtype),
            *[pltpu.VMEM((channels, blocks, PAD + rows + SUB, LANES), f32)] * SWEEPS,
            pltpu.VMEM((channels, blocks, rows, LANES), f32),
            pltpu.VMEM((channels, blocks, rows, LANES), f32),
            pltpu.VMEM((blocks, rows, LANES), f32),
            pltpu.VMEM((channels, blocks, PAD + rows, LANES), f32),
            pltpu.VMEM((channels, blocks, PAD + rows, LANES), f32),
            pltpu.VMEM((2, channels, rows, LANES), f32),
            pltpu.VMEM((channels, rows, LANES), f32),
            pltpu.VMEM((SUB, LANES), f32),
            pltpu.VMEM((n, SUB, LANES), f32),
            pltpu.VMEM((channels, band_blocks, band_rows, LANES), f32),
            pltpu.VMEM((channels, band_blocks, band_rows, LANES), f32),
            pltpu.SemaphoreType.DMA((SWEEPS, 2)),
            pltpu.SemaphoreType.DMA((SWEEPS, 2)),
            pltpu.SemaphoreType.DMA((2,)),
            pltpu.SemaphoreType.DMA((2,)),
            pltpu.SemaphoreType.DMA((n,)),
            pltpu.SemaphoreType.DMA((n,)),
            pltpu.SemaphoreType.DMA((2,)),
            pltpu.SemaphoreType.DMA((4,)),
        ],
        compiler_params=pltpu.CompilerParams(
            collective_id=0, has_side_effects=True, vmem_limit_bytes=50 * 2**20
        ),
    )(image, grad_x, grad_y, classes, validity, jnp.swapaxes(owners, 1, 2))


def solution(mesh):
    in_specs = (
        P(None, ("win", "row"), None),
        P(None, ("win", "row"), None),
        P(None, ("win", "row"), None),
        P(("win", "row"), None),
        P("win", None),
        P("win", None, None),
    )
    out_specs = P(None, ("win", "row"), None)
    return jax.shard_map(
        per_device, mesh=mesh, in_specs=in_specs, out_specs=out_specs, check_vma=False
    )
```

```python
import functools

import jax
import jax.numpy as jnp
from jax import lax
from jax.experimental import pallas as pl
from jax.experimental.pallas import tpu as pltpu
from jax.sharding import PartitionSpec as P

TILE_ROWS = 1024
TILE_COLS = 1024
BAND = 48
SWEEPS = 4
OMEGA = 0.8
SCREEN = 0.25
LANES = 128
SUB = 8
PAD = 8
MESH = pl.DeviceIdType.MESH
AHEAD = 6


def kernel(
    n, image_in, gx_in, gy_in, classes_in, validity, owners, out,
    image, grad_x, grad_y, classes, s0, s1, s2, s3, d_term, a_term, b_term, gxf, gyf, sums, level, tot, gathered, band_out, band_in,
    halo_send, halo_recv, grad_send, grad_recv, tot_send, tot_recv, band_sems, in_sems,
):
    channels, rows, width = image_in.shape
    blocks, tiles = width // LANES, rows // SUB
    per_tile = TILE_COLS // LANES
    seams_below = validity.shape[0] > 1
    pos = lax.axis_index("row")
    win = lax.axis_index("win")
    tile_row = pos * rows // TILE_ROWS
    lane = lax.broadcasted_iota(jnp.int32, (SUB, LANES), 1)
    lane16 = lax.broadcasted_iota(jnp.int32, (2 * SUB, LANES), 1)
    first_lane, last_lane = lane == 0, lane == LANES - 1
    zero = jnp.zeros((SUB, LANES), jnp.float32)
    has_above, has_below = pos > 0, pos < n - 1

    iterates = (s0, s1, s2, s3)
    fetch_gy, fetch_gx, fetch_image, fetch_classes = (
        pltpu.make_async_copy(src, dst, in_sems.at[q])
        for q, (src, dst) in enumerate(
            ((gy_in, grad_y), (gx_in, grad_x), (image_in, image), (classes_in, classes))
        )
    )
    for fetch in (fetch_gy, fetch_gx, fetch_image, fetch_classes):
        fetch.start()

    barrier = pltpu.get_barrier_semaphore()

    def greet(j, carry):
        @pl.when((j < pos) | (j == pos + 1))
        def _():
            pl.semaphore_signal(barrier, inc=1, device_id=(win, j), device_id_type=MESH)
        return carry

    lax.fori_loop(0, n, greet, 0)

    def remote(src, dst, send, recv, to):
        return pltpu.make_async_remote_copy(
            src_ref=src, dst_ref=dst, send_sem=send, recv_sem=recv,
            device_id=(win, to), device_id_type=MESH,
        )

    def row_of(ref, row):
        return ref.at[:, :, pl.ds(row, 1), :]

    def gy_pass(j, carry):
        k, at = j // (tiles // 2), (j % (tiles // 2)) * 2 * SUB
        total = [None, None]
        for c in range(blocks):
            v = grad_y[k, pl.ds(at, 2 * SUB), c * LANES:(c + 1) * LANES].astype(jnp.float32)
            gyf[k, c, pl.ds(PAD + at, 2 * SUB), :] = v
            total[c % 2] = v if total[c % 2] is None else total[c % 2] + v
        sums[0, k, pl.ds(at, 2 * SUB), :] = total[0] + total[1]
        return carry

    fetch_gy.wait()
    lax.fori_loop(0, channels * tiles // 2, gy_pass, 0)

    def gx_pass(j, carry):
        k, at = j // (tiles // 2), (j % (tiles // 2)) * 2 * SUB
        for c in range(blocks):
            v = grad_x[k, pl.ds(at, 2 * SUB), c * LANES:(c + 1) * LANES].astype(jnp.float32)
            if (c + 1) % per_tile == 0 and c + 1 < blocks:
                after = grad_x[k, pl.ds(at, 2 * SUB), (c + 1) * LANES:(c + 2) * LANES].astype(jnp.float32)
                inside = (lane16 >= LANES - 1 - BAND) & (lane16 < LANES - 1)
                left = jnp.sum(jnp.where(inside, v, 0.0), axis=1, keepdims=True)
                right = jnp.sum(jnp.where(lane16 < BAND, after, 0.0), axis=1, keepdims=True)
                owns = owners[tile_row, 1, c // per_tile] == 1
                mean = jnp.where(owns, right, left) * (1.0 / BAND)
                v = jnp.where(lane16 == LANES - 1, mean, v)
            gxf[k, c, pl.ds(PAD + at, 2 * SUB), :] = v
        return carry

    fetch_gx.wait()
    lax.fori_loop(0, channels * tiles // 2, gx_pass, 0)

    pl.semaphore_wait(barrier, n - 1 - pos + jnp.where(has_above, 1, 0))

    if seams_below:
        def band_pass(j, carry):
            k, c = j // blocks, j % blocks
            mean = jnp.sum(gyf[k, c, PAD:PAD + BAND, :], axis=0, keepdims=True) * (1.0 / BAND)
            band_out[k, c] = jnp.broadcast_to(mean, (SUB, LANES))
            return carry

        lax.fori_loop(0, channels * blocks, band_pass, 0)
        band = remote(row_of(band_out, 0), row_of(band_in, 0), band_sems.at[0], band_sems.at[1], pos - 1)

        @pl.when(has_above)
        def _():
            band.start()

        @pl.when(has_below)
        def _():
            band.wait_recv()

        @pl.when(has_above)
        def _():
            band.wait_send()

        at_seam = has_below & ((pos + 1) * rows % TILE_ROWS == 0)

        @pl.when(at_seam)
        def _():
            last = PAD + rows - 1
            for k in range(channels):
                total = jnp.zeros((1, LANES), jnp.float32)
                for c in range(blocks):
                    upper = jnp.sum(gyf[k, c, last - BAND:last, :], axis=0, keepdims=True) * (1.0 / BAND)
                    owns = owners[tile_row, 0, c // per_tile] == 1
                    new = jnp.where(owns, band_in[k, c, 0:1, :], upper)
                    gyf[k, c, last:last + 1, :] = new
                    total = total + new
                sums[0, k, rows - 1:rows, :] = total

    grads = [
        remote(row_of(g, PAD + rows - 1), row_of(g, PAD - 1), grad_send.at[q], grad_recv.at[q], pos + 1)
        for q, g in enumerate((gxf, gyf))
    ]

    @pl.when(has_below)
    def _():
        for copy in grads:
            copy.start()

    fetch_image.wait()
    tot[...] = zero
    for k in range(channels):
        first = image[k, 0:SUB, 0:LANES]
        for c in range(1, blocks):
            first = first + image[k, 0:SUB, c * LANES:(c + 1) * LANES]
        mean = jnp.sum(first, axis=1, keepdims=True) * (1.0 / width)
        tot[channels + k:channels + k + 1, :] = jnp.broadcast_to(mean[0:1], (1, LANES))
        my = jnp.sum(sums[0, k], axis=1, keepdims=True) * (1.0 / width)
        sums[0, k] = jnp.broadcast_to(my, (rows, LANES))
        tot[k:k + 1, :] = jnp.broadcast_to(jnp.sum(my, axis=0, keepdims=True), (1, LANES))

    def tell(j, carry):
        @pl.when(j > pos)
        def _():
            remote(tot, gathered.at[pos], tot_send.at[j], tot_recv.at[pos], j).start()
        return carry

    lax.fori_loop(0, n, tell, 0)

    @pl.when(jnp.logical_not(has_above))
    def _():
        for k in range(channels):
            for c in range(blocks):
                gxf[k, c, PAD - 1:PAD, :] = zero[:1]
                gyf[k, c, PAD - 1:PAD, :] = zero[:1]
                for t in range(SWEEPS):
                    iterates[t][k, c, PAD - 1:PAD, :] = zero[:1]

    @pl.when(jnp.logical_not(has_below))
    def _():
        for k in range(channels):
            for c in range(blocks):
                for t in range(SWEEPS):
                    iterates[t][k, c, PAD + rows:PAD + rows + 1, :] = zero[:1]

    def image_pass(j, carry):
        k, at = j // tiles, (j % tiles) * SUB
        total = [None, None]
        for c in range(blocks):
            v = image[k, pl.ds(at, SUB), c * LANES:(c + 1) * LANES]
            total[c % 2] = v if total[c % 2] is None else total[c % 2] + v
        sums[1, k, pl.ds(at, SUB), :] = total[0] + total[1]
        return carry

    lax.fori_loop(0, channels * tiles, image_pass, 0)

    def weight_pass(i, carry):
        at = i * SUB
        for c in range(blocks):
            power = (1 << classes[pl.ds(at, SUB), c * LANES:(c + 1) * LANES]).astype(jnp.float32)
            cover = validity[tile_row, c // per_tile].astype(jnp.float32) * SCREEN
            b_term[c, pl.ds(at, SUB), :] = OMEGA / (cover * power + 6.0)
        return carry

    fetch_classes.wait()
    lax.fori_loop(0, tiles, weight_pass, 0)

    def div_tile(k, i):
        at = i * SUB
        state = []

        def load(c):
            x0, xm = gxf[k, c, pl.ds(PAD + at, SUB), :], gxf[k, c, pl.ds(PAD - 1 + at, SUB), :]
            y0, ym = gyf[k, c, pl.ds(PAD + at, SUB), :], gyf[k, c, pl.ds(PAD - 1 + at, SUB), :]
            x = 1.5 * x0 + 0.5 * xm
            y = 0.5 * y0
            return x + y0 - 2.0 * ym, pltpu.roll(y - x, 1, 1), pltpu.roll(y, LANES - 1, 1)

        before, ready = zero, [load(c) for c in range(min(AHEAD, blocks))]
        for c in range(blocks):
            if c + AHEAD < blocks:
                ready.append(load(c + AHEAD))
            here = ready.pop(0)
            after = ready[0] if ready else (None, None, zero)
            base, left, right = here
            moved = jnp.where(first_lane, before, left) + jnp.where(last_lane, after[2], right)
            d_term[k, c, pl.ds(at, SUB), :] = b_term[c, pl.ds(at, SUB), :] * (base + moved)
            before = left

    def div_loop(j, carry):
        div_tile(j // (tiles - 1), 1 + j % (tiles - 1))
        return carry

    lax.fori_loop(0, channels * (tiles - 1), div_loop, 0)

    @pl.when(has_above)
    def _():
        for copy in grads:
            copy.wait_recv()

    def div_first(k, carry):
        div_tile(k, 0)
        return carry

    lax.fori_loop(0, channels, div_first, 0)

    down = lax.broadcasted_iota(jnp.int32, (rows, rows), 0)
    across = lax.broadcasted_iota(jnp.int32, (rows, rows), 1)
    strictly = (across < down).astype(jnp.float32)
    for k in range(channels):
        running = jnp.dot(
            strictly, sums[0, k], precision=lax.Precision.HIGHEST, preferred_element_type=jnp.float32
        )
        mf = jnp.sum(sums[1, k], axis=1, keepdims=True) * (1.0 / width)
        level[k] = running - mf

    gathered[pos] = tot[...]

    def hear(j, carry):
        @pl.when(j < pos)
        def _():
            remote(tot, gathered.at[j], tot_send.at[j], tot_recv.at[j], j).wait_recv()
        return carry

    lax.fori_loop(0, n, hear, 0)
    before = lax.fori_loop(0, pos, lambda j, total: total + gathered[j], zero)
    leading = gathered[0]
    for k in range(channels):
        level[k] = level[k] + (before[k:k + 1, :] + leading[channels + k:channels + k + 1, :])

    def start_tile(k, i):
        at = i * SUB
        up = level[k, pl.ds(at, SUB), :]
        for c in range(blocks):
            target = image[k, pl.ds(at, SUB), c * LANES:(c + 1) * LANES] + up
            s0[k, c, pl.ds(PAD + at, SUB), :] = target
            rest = OMEGA - 6.0 * b_term[c, pl.ds(at, SUB), :]
            a_term[k, c, pl.ds(at, SUB), :] = rest * target - d_term[k, c, pl.ds(at, SUB), :]

    def sweep_tile(t, k, i):
        at = i * SUB

        def load(c):
            mid = iterates[t][k, c, pl.ds(PAD + at, SUB), :]
            v = iterates[t][k, c, pl.ds(PAD - 1 + at, SUB), :] + iterates[t][k, c, pl.ds(PAD + 1 + at, SUB), :]
            q = mid + 0.5 * v
            return mid, v, pltpu.roll(q, 1, 1), pltpu.roll(q, LANES - 1, 1)

        before, ready = zero, [load(c) for c in range(min(AHEAD, blocks))]
        for c in range(blocks):
            if c + AHEAD < blocks:
                ready.append(load(c + AHEAD))
            here = ready.pop(0)
            after = ready[0] if ready else (None, None, None, zero)
            mid, v, left, right = here
            around = v + jnp.where(first_lane, before, left) + jnp.where(last_lane, after[3], right)
            new = (1.0 - OMEGA) * mid + (
                a_term[k, c, pl.ds(at, SUB), :] + b_term[c, pl.ds(at, SUB), :] * around
            )
            if t + 1 < SWEEPS:
                iterates[t + 1][k, c, pl.ds(PAD + at, SUB), :] = new
            else:
                out[k, pl.ds(at, SUB), c * LANES:(c + 1) * LANES] = new
            before = left

    def halo(t):
        up = remote(row_of(iterates[t], PAD), row_of(iterates[t], PAD + rows), halo_send.at[t, 0], halo_recv.at[t, 0], pos - 1)
        dn = remote(row_of(iterates[t], PAD + rows - 1), row_of(iterates[t], PAD - 1), halo_send.at[t, 1], halo_recv.at[t, 1], pos + 1)
        return up, dn

    def rim_then_inner(work, t):
        def rim(j, carry):
            work(j // 2, (j % 2) * (tiles - 1))
            return carry

        def inner(j, carry):
            work(j // (tiles - 2), 1 + j % (tiles - 2))
            return carry

        lax.fori_loop(0, channels * 2, rim, 0)
        if t < SWEEPS:
            up, dn = halo(t)

            @pl.when(has_above)
            def _():
                up.start()

            @pl.when(has_below)
            def _():
                dn.start()

        lax.fori_loop(0, channels * (tiles - 2), inner, 0)
        if t < SWEEPS:
            @pl.when(has_below)
            def _():
                up.wait_recv()

            @pl.when(has_above)
            def _():
                dn.wait_recv()

    rim_then_inner(start_tile, 0)
    for t in range(SWEEPS):
        rim_then_inner(functools.partial(sweep_tile, t), t + 1)

    for t in range(SWEEPS):
        up, dn = halo(t)

        @pl.when(has_above)
        def _():
            up.wait_send()

        @pl.when(has_below)
        def _():
            dn.wait_send()

    @pl.when(has_below)
    def _():
        for copy in grads:
            copy.wait_send()

    def sent(j, carry):
        @pl.when(j > pos)
        def _():
            remote(tot, gathered.at[pos], tot_send.at[j], tot_recv.at[pos], j).wait_send()
        return carry

    lax.fori_loop(0, n, sent, 0)


def per_device(image, grad_x, grad_y, classes, validity, owners):
    n = lax.axis_size("row")
    channels, rows, width = image.shape
    blocks = width // LANES
    vmem, smem = pl.BlockSpec(memory_space=pltpu.VMEM), pl.BlockSpec(memory_space=pltpu.SMEM)
    f32 = jnp.float32
    band_rows = SUB if validity.shape[0] > 1 else 1
    band_blocks = blocks if validity.shape[0] > 1 else 1
    return pl.pallas_call(
        functools.partial(kernel, n),
        out_shape=pltpu.VMEM(image.shape, f32),
        in_specs=[pl.BlockSpec(memory_space=pl.ANY)] * 4 + [smem] * 2,
        out_specs=vmem,
        scratch_shapes=[
            pltpu.VMEM(image.shape, image.dtype),
            pltpu.VMEM(grad_x.shape, grad_x.dtype),
            pltpu.VMEM(grad_y.shape, grad_y.dtype),
            pltpu.VMEM(classes.shape, classes.dtype),
            *[pltpu.VMEM((channels, blocks, PAD + rows + SUB, LANES), f32)] * SWEEPS,
            pltpu.VMEM((channels, blocks, rows, LANES), f32),
            pltpu.VMEM((channels, blocks, rows, LANES), f32),
            pltpu.VMEM((blocks, rows, LANES), f32),
            pltpu.VMEM((channels, blocks, PAD + rows, LANES), f32),
            pltpu.VMEM((channels, blocks, PAD + rows, LANES), f32),
            pltpu.VMEM((2, channels, rows, LANES), f32),
            pltpu.VMEM((channels, rows, LANES), f32),
            pltpu.VMEM((SUB, LANES), f32),
            pltpu.VMEM((n, SUB, LANES), f32),
            pltpu.VMEM((channels, band_blocks, band_rows, LANES), f32),
            pltpu.VMEM((channels, band_blocks, band_rows, LANES), f32),
            pltpu.SemaphoreType.DMA((SWEEPS, 2)),
            pltpu.SemaphoreType.DMA((SWEEPS, 2)),
            pltpu.SemaphoreType.DMA((2,)),
            pltpu.SemaphoreType.DMA((2,)),
            pltpu.SemaphoreType.DMA((n,)),
            pltpu.SemaphoreType.DMA((n,)),
            pltpu.SemaphoreType.DMA((2,)),
            pltpu.SemaphoreType.DMA((4,)),
        ],
        compiler_params=pltpu.CompilerParams(
            collective_id=0, has_side_effects=True, vmem_limit_bytes=50 * 2**20
        ),
    )(image, grad_x, grad_y, classes, validity, jnp.swapaxes(owners, 1, 2))


def solution(mesh):
    in_specs = (
        P(None, ("win", "row"), None),
        P(None, ("win", "row"), None),
        P(None, ("win", "row"), None),
        P(("win", "row"), None),
        P("win", None),
        P("win", None, None),
    )
    out_specs = P(None, ("win", "row"), None)
    return jax.shard_map(
        per_device, mesh=mesh, in_specs=in_specs, out_specs=out_specs, check_vma=False
    )
```
